32 devices in a mesh: tok: 8 (over z, y), hid: 4 (over x, core).
Axes of the slice: x: 2, y: 2, z: 4, core: 2. Of those that a mesh axis runs over, the one named last changes fastest.
Arguments:
- queries: bfloat16 [2048, 5120], P('tok', 'hid'), may hold values from -40 to 40
- keys: bfloat16 [2048, 5120], P('tok', 'hid'), may hold values from -40 to 40
- values: bfloat16 [2048, 5120], P('tok', 'hid'), may hold values from -6 to 6
- residual: bfloat16 [2048, 5120], P('tok', 'hid'), may hold values from -62 to 62
- out_weight: bfloat16 [5120, 5120], P(None, 'hid'), may hold values from -0.078125 to 0.078125
- adapter_a: bfloat16 [64, 5120, 16], P('tok', 'hid'), may hold values from -0.078125 to 0.078125
- adapter_b: bfloat16 [64, 16, 5120], P('tok', None, 'hid'), may hold values from -1.5 to 1.5
- request_lengths: int32 [4], replicated, may hold values from 256 to 768, as said below
- request_adapter: int32 [4], replicated, may hold values from 0 to 63
- adapter_slot: int32 [64], replicated, may hold values from 0 to 63, each once
- mod_scale: float32 [5120], P('hid'), may hold values from -3 to 3
- mod_shift: float32 [5120], P('hid'), may hold values from -3 to 3
Outputs:
- stream: bfloat16 [2048, 5120], P('tok', 'hid')
- normed: bfloat16 [2048, 5120], P('tok', 'hid')
The draws below stay inside these ranges and needn't reach their ends.
Inputs may be any that keep to these rules, and one draw needn't show every extreme that they name: `request_lengths`: each request holds 256 to 768 tokens, together all 2048; some request holds exactly 768. `adapter_slot`: each slot once.
All inputs are finite; a program needn't handle non-finite values.
Results may differ from the reference program's by a relative error of at most 0.0027.
Values may be sent and summed in bfloat16 or wider, within the bound.
A program may use at most 128 MiB of HBM per device.

```python
import math
import jax
import jax.numpy as jnp
from jax import lax

HEADS = 40
HEAD_DIM = 128
D = 5120
RANK = 16
ADAPTERS = 64
TOK_DEV = 256
REACH = 3
TOKENS = 2048
REQUESTS = 4
MOST = 768


def paired_draw(key):
    base_q = jnp.clip(jax.random.normal(jax.random.fold_in(key, 101), (TOKENS, D), jnp.float32), -6.0, 6.0)
    base_k = jnp.clip(jax.random.normal(jax.random.fold_in(key, 102), (TOKENS, D), jnp.float32), -6.0, 6.0)
    return (base_q, base_k)


def draw_queries(key, part):
    return paired_draw(key)[0].astype(jnp.bfloat16)


def draw_keys(key, part):
    return paired_draw(key)[1].astype(jnp.bfloat16)


def draw_residual(key, part):
    column = jnp.arange(D, dtype=jnp.float32) / (D - 1)
    entries = jnp.clip(jax.random.normal(jax.random.fold_in(key, 203), (TOKENS, D), jnp.float32), -6.0, 6.0)
    return (entries * jnp.exp(math.log(3.0) * column)[None, :]).astype(jnp.bfloat16)


def draw_request_lengths(key, part):
    key = jax.random.fold_in(key, 300)
    count = REQUESTS
    block = TOK_DEV
    longest = MOST
    offset = jax.random.randint(jax.random.fold_in(key, 1), (), 1, block, dtype=jnp.int32)
    if count >= 5:
        forced = 2
        first = jax.random.randint(jax.random.fold_in(key, 2), (), 2, count - 2, dtype=jnp.int32)
        start = (2 * block * (first - 1) + offset).astype(jnp.int32)
    else:
        forced = 1
        first = jnp.int32(1)
        start = (2 * block + offset).astype(jnp.int32)
    after_total = (TOKENS - start - forced * longest).astype(jnp.int32)
    after_count = (count - first - forced).astype(jnp.int32)
    stepkey = jax.random.fold_in(key, 3)

    def step(carry, index):
        remain, left = carry
        reset = index == first + forced
        remain = jnp.where(reset, after_total, remain).astype(jnp.int32)
        left = jnp.where(reset, after_count, left).astype(jnp.int32)
        pinned = (index >= first) & (index < first + forced)
        lowest = jnp.maximum(block, remain - longest * (left - 1)).astype(jnp.int32)
        highest = jnp.minimum(longest, remain - block * (left - 1)).astype(jnp.int32)
        highest = jnp.maximum(highest, lowest)
        picked = jax.random.randint(jax.random.fold_in(stepkey, index), (), lowest, highest + 1, dtype=jnp.int32)
        length = jnp.where(pinned, longest, picked).astype(jnp.int32)
        remain = jnp.where(pinned, remain, remain - picked).astype(jnp.int32)
        left = jnp.where(pinned, left, left - 1).astype(jnp.int32)
        return ((remain, left), length)
    carry_start = (start, first.astype(jnp.int32))
    carry_end, lengths = lax.scan(step, carry_start, jnp.arange(count, dtype=jnp.int32))
    return lengths.astype(jnp.int32)


def set_ends(drawn, own_key, least, top_value):
    longest = drawn.shape.index(max(drawn.shape))
    spots = []
    for shift in (0, 1):
        where = [jax.random.randint(jax.random.fold_in(own_key, axis), (), 0, length) for axis, length in enumerate(drawn.shape)]
        where[longest] = (where[longest] + shift) % drawn.shape[longest]
        spots.append(tuple(where))
    return drawn.at[spots[0]].set(least).at[spots[1]].set(top_value)


def steps_of(rng, extent, cuts, least, largest):
    level = 1.0
    for position, shards_of in cuts:
        steps = jax.random.uniform(jax.random.fold_in(jax.random.fold_in(rng, 6), position), (shards_of,), jnp.float32, least / len(cuts), largest / len(cuts))
        level = level * jnp.repeat(jnp.exp(steps), extent[position] // shards_of).reshape((-1,) + (1,) * (len(extent) - 1 - position))
    return level


def gaussian(rng, extent, width, reach, split=(), kind=jnp.bfloat16):
    gain = steps_of(rng, extent, split, -0.22, 0.18) if split else 1.0
    values = jax.random.normal(rng, extent, jnp.float32) * width * gain
    return jnp.minimum(jnp.maximum(values, -reach), reach).astype(kind)


def setup_inputs(seed: int = 0) -> dict:
    key_of = jax.random.split(jax.random.key(seed), 13)
    return {
        "queries": draw_queries(jax.random.fold_in(key_of[12], 71), 0),
        "keys": draw_keys(jax.random.fold_in(key_of[12], 71), 0),
        "values": gaussian(key_of[2], (TOKENS, D), 1.0, 6.0, ((0, 8), (1, 4))),
        "residual": draw_residual(jax.random.fold_in(key_of[12], 71), 0),
        "out_weight": gaussian(key_of[4], (D, D), D ** -0.5, 0.078125, ((1, 4),)),
        "adapter_a": gaussian(key_of[5], (ADAPTERS, D, RANK), D ** -0.5, 0.078125, ((0, 8), (1, 4))),
        "adapter_b": gaussian(key_of[6], (ADAPTERS, RANK, D), RANK ** -0.5, 1.5, ((0, 8), (2, 4))),
        "request_lengths": draw_request_lengths(jax.random.fold_in(key_of[12], 71), 0),
        "request_adapter": set_ends(jax.random.randint(key_of[8], (REQUESTS,), 0, ADAPTERS), jax.random.fold_in(key_of[8], 1), 0, ADAPTERS - 1).astype(jnp.int32),
        "adapter_slot": jax.random.permutation(key_of[9], ADAPTERS).astype(jnp.int32),
        "mod_scale": gaussian(key_of[10], (D,), 0.5, 3.0, ((0, 4),), jnp.float32),
        "mod_shift": gaussian(key_of[11], (D,), 0.5, 3.0, ((0, 4),), jnp.float32),
    }


def segments_of(positions, request_lengths):
    ends = jnp.cumsum(request_lengths)
    return lax.optimization_barrier(jnp.sum((ends[None, :] <= positions[:, None]).astype(jnp.int32), axis=1)).astype(jnp.int32)

def reference(queries, keys, values, residual, out_weight, adapter_a, adapter_b, request_lengths, request_adapter, adapter_slot, mod_scale, mod_shift):
    total_rows = queries.shape[0]
    block = TOK_DEV
    margin = REACH * TOK_DEV
    positions = jnp.arange(total_rows, dtype=jnp.int32)
    segment = segments_of(positions, request_lengths)
    slot_of_request = adapter_slot[request_adapter]
    slot = slot_of_request[jnp.minimum(segment, REQUESTS - 1)]
    key_pad = jnp.pad(keys.astype(jnp.float32), ((margin, margin), (0, 0)))
    val_pad = jnp.pad(values.astype(jnp.float32), ((margin, margin), (0, 0)))
    seg_pad = jnp.pad(segment, (margin, margin), constant_values=-1).astype(jnp.int32)
    span = block + 2 * margin

    def one_block(index):
        start = (index * block).astype(jnp.int32)
        query_block = lax.dynamic_slice_in_dim(queries, start, block, 0).astype(jnp.float32).reshape(block, HEADS, HEAD_DIM)
        key_block = lax.dynamic_slice_in_dim(key_pad, start, span, 0).reshape(span, HEADS, HEAD_DIM)
        val_block = lax.dynamic_slice_in_dim(val_pad, start, span, 0).reshape(span, HEADS, HEAD_DIM)
        query_seg = lax.dynamic_slice_in_dim(segment, start, block, 0)
        key_seg = lax.dynamic_slice_in_dim(seg_pad, start, span, 0)
        scores = jnp.einsum('qhd,khd->hqk', query_block, key_block) / math.sqrt(HEAD_DIM)
        admit = (query_seg[:, None] == key_seg[None, :])[None, :, :]
        scores = jnp.where(admit, scores, -1e+30)
        top = lax.optimization_barrier(jnp.max(scores, axis=-1, keepdims=True))
        expo = jnp.exp(scores - top)
        weights = (expo / lax.optimization_barrier(jnp.sum(expo, axis=-1, keepdims=True))).astype(jnp.bfloat16)
        out = jnp.einsum('hqk,khd->qhd', weights.astype(jnp.float32), val_block)
        return out.astype(jnp.bfloat16).reshape(block, D)
    attended = lax.map(one_block, jnp.arange(total_rows // block, dtype=jnp.int32)).reshape(total_rows, D)
    projected = jnp.dot(attended, out_weight, preferred_element_type=jnp.float32)
    bank_down = adapter_a.transpose(1, 0, 2).reshape(D, ADAPTERS * RANK)
    wide = jnp.dot(attended, bank_down, preferred_element_type=jnp.float32).reshape(total_rows, ADAPTERS, RANK)
    onehot = (slot[:, None] == jnp.arange(ADAPTERS, dtype=jnp.int32)[None, :]).astype(jnp.float32)
    down = lax.optimization_barrier(jnp.sum(onehot[:, :, None] * wide, axis=1)).astype(jnp.bfloat16)
    expand = (onehot.astype(jnp.bfloat16)[:, :, None] * down[:, None, :]).reshape(total_rows, ADAPTERS * RANK)
    lift = jnp.dot(expand, adapter_b.reshape(ADAPTERS * RANK, D), preferred_element_type=jnp.float32)
    total = residual.astype(jnp.float32) + projected + lift
    stream = total.astype(jnp.bfloat16)
    mean = lax.optimization_barrier(jnp.mean(total, axis=-1, keepdims=True))
    centered = total - mean
    variance = lax.optimization_barrier(jnp.mean(centered * centered, axis=-1, keepdims=True))
    normed = (centered / jnp.sqrt(variance + 1e-06) * (1.0 + mod_scale) + mod_shift).astype(jnp.bfloat16)
    return (stream, normed)
```

```python
import functools
import math

import jax
import jax.numpy as jnp
from jax import lax
from jax.experimental import pallas as pl
from jax.experimental.pallas import tpu as pltpu
from jax.sharding import PartitionSpec as P

HEAD_DIM = 128
D = 5120
MESH = pl.DeviceIdType.MESH
NT = (((1,), (1,)), ((), ()))


def segment_of(pos, len_ref, requests):
    end = jnp.int32(0)
    seg = jnp.zeros_like(pos)
    for r in range(requests):
        end = end + len_ref[r]
        seg = seg + (pos >= end).astype(jnp.int32)
    return jnp.where(pos < 0, -1, seg)


def greet(targets):
    barrier = pltpu.get_barrier_semaphore()
    count = jnp.int32(0)
    for cond, dev in targets:

        def signal(dev=dev):
            pl.semaphore_signal(barrier, inc=1, device_id=dev, device_id_type=MESH)

        if cond is None:
            signal()
            count = count + 1
        else:
            pl.when(cond)(signal)
            count = count + cond.astype(jnp.int32)
    pl.semaphore_wait(barrier, count)


def run(cond, fn):
    if cond is None:
        fn()
    else:
        pl.when(cond)(fn)


def attention_kernel(
    n_tok, n_hid, requests,
    q_ref, k_ref, v_ref, w_ref, len_ref,
    acc_ref, att_ref,
    qb, kv, ag, wb, ob,
    w_sem, l_sem, ys, yr, zs, zr, ps, pr, fs, fr, as_, ar, hs, hr,
):
    rows, local = q_ref.shape
    hc = HEAD_DIM
    per = local // hc // 2
    tok, h = lax.axis_index("tok"), lax.axis_index("hid")
    p, y = tok // 2, tok % 2
    levels = n_tok // 2
    partner = (2 * p + 1 - y, h)
    up, down = (tok + 2, h), (tok - 2, h)
    has_up, has_down = p < levels - 1, p > 0
    others = [(tok, lax.rem(h + d, n_hid)) for d in range(1, n_hid)]
    greet([(None, partner), (has_up, up), (has_down, down)] + [(None, o) for o in others])

    own = pl.multiple_of(y * rows, rows)
    oth = pl.multiple_of((1 - y) * rows, rows)
    own_cols = y * (per * hc)
    oth_cols = (1 - y) * (per * hc)
    base = 3 * rows
    sends = []

    def remote(src, dst, ss, rs, dev):
        return pltpu.make_async_remote_copy(
            src_ref=src, dst_ref=dst, send_sem=ss, recv_sem=rs, device_id=dev, device_id_type=MESH
        )

    def go(cond, copy):
        run(cond, lambda: copy.start())
        sends.append((cond, copy))

    def cols(start, j):
        return pl.ds(pl.multiple_of(start + j * hc, hc), hc)

    ways = [(has_up, up, base - 2 * rows, has_down), (has_down, down, base + 2 * rows, has_up)]

    y_copies, l_copies, z_copies = [], [], []
    for j in range(per):
        yc, lc, zc = [], [], []
        for i, (ref, at) in enumerate(((k_ref, kv), (v_ref, kv), (q_ref, qb))):
            src = ref.at[:, cols(oth_cols, j)]
            mine = ref.at[:, cols(own_cols, j)]
            dst = kv.at[j, i, pl.ds(base + own, rows), :] if i < 2 else qb.at[j, pl.ds(own, rows), :]
            c = remote(src, dst, ys.at[j, i], yr.at[j, i], partner)
            go(None, c)
            yc.append(c)
            c = pltpu.make_async_copy(mine, dst, l_sem.at[j, i])
            c.start()
            lc.append(c)
            if i < 2:
                for w, (cond, dev, first, rcond) in enumerate(ways):
                    c = remote(
                        mine, kv.at[j, i, pl.ds(first + own, rows), :], zs.at[j, w, i], zr.at[j, w, i], dev
                    )
                    go(cond, c)
                    zc.append((rcond, c))
        y_copies.append(yc)
        l_copies.append(lc)
        z_copies.append(zc)

    w_copies = []
    for j in range(per):
        wc = []
        for g in range(2 * n_hid):
            row = (g // 2) * local + (g % 2) * per * hc + j * hc
            c = pltpu.make_async_copy(
                w_ref.at[pl.ds(row, hc), :], wb.at[j, pl.ds(g * hc, hc), :], w_sem.at[j, g]
            )
            c.start()
            wc.append(c)
        w_copies.append(wc)

    @pl.when(p == 0)
    def _():
        kv[:, :, 0 : 3 * rows, :] = jnp.zeros((per, 2, 3 * rows, hc), kv.dtype)

    @pl.when(p == 1)
    def _():
        kv[:, :, 0:rows, :] = jnp.zeros((per, 2, rows, hc), kv.dtype)

    @pl.when(p == levels - 1)
    def _():
        kv[:, :, 5 * rows : 8 * rows, :] = jnp.zeros((per, 2, 3 * rows, hc), kv.dtype)

    @pl.when(p == levels - 2)
    def _():
        kv[:, :, 7 * rows : 8 * rows, :] = jnp.zeros((per, 2, rows, hc), kv.dtype)

    p_copies = []

    def stage_a(j):
        for c in y_copies[j]:
            c.wait_recv()
        pc = []
        for w, (cond, dev, first, rcond) in enumerate(ways):
            c = remote(
                kv.at[j, :, pl.ds(base + oth, rows), :],
                kv.at[j, :, pl.ds(first + oth, rows), :],
                ps.at[j, w], pr.at[j, w], dev,
            )
            go(cond, c)
            pc.append((rcond, c))
        p_copies.append(pc)

    f_copies = []
    fwd = [
        (has_up & has_down, up, 2 * rows, 0, p > 1),
        (has_up & has_down, down, 5 * rows, 7 * rows, p < levels - 2),
    ]

    def stage_b(j):
        fc = []
        for w, (cond, dev, src, dst, rcond) in enumerate(fwd):
            for rc, c in z_copies[j][w::2] + p_copies[j][w : w + 1]:
                run(rc, lambda c=c: c.wait_recv())
            c = remote(
                kv.at[j, :, pl.ds(src, rows), :], kv.at[j, :, pl.ds(dst, rows), :],
                fs.at[j, w], fr.at[j, w], dev,
            )
            go(cond, c)
            fc.append((rcond, c))
        f_copies.append(fc)

    scale = math.log2(math.e) / math.sqrt(HEAD_DIM)
    tile = 128
    span = 7 * rows

    def attend(j, first, store):
        level_pos = p * (2 * rows)
        kseg = segment_of(
            level_pos - base + first + lax.broadcasted_iota(jnp.int32, (1, span), 1), len_ref, requests
        )

        def body(t, carry):
            at = pl.multiple_of(t * tile, tile)
            qseg = segment_of(
                level_pos + first + at + lax.broadcasted_iota(jnp.int32, (tile, 1), 0), len_ref, requests
            )
            q = qb[j, pl.ds(first + at, tile), :]
            s = lax.dot_general(
                q, kv[j, 0, pl.ds(first, span), :], NT, preferred_element_type=jnp.float32
            )
            s = jnp.where(qseg == kseg, s, -1e30)
            top = jnp.max(s, axis=1, keepdims=True)
            e = jnp.exp2((s - top) * scale)
            total = jnp.sum(e, axis=1, keepdims=True)
            o = jnp.dot(
                e.astype(jnp.bfloat16), kv[j, 1, pl.ds(first, span), :], preferred_element_type=jnp.float32
            )
            store(at, (o / total).astype(jnp.bfloat16))
            return carry

        lax.fori_loop(0, rows // tile, body, 0)

    a_copies = []
    my_col = pl.ds(pl.multiple_of((h * 2 + y) * hc, hc), hc)

    def stage_c(j):
        for c in l_copies[j]:
            c.wait()
        for rc, c in f_copies[j]:
            run(rc, lambda c=c: c.wait_recv())

        def store_other(at, o):
            ob[j, pl.ds(at, tile), :] = o

        def store_own(at, o):
            ag[j, pl.ds(at, tile), my_col] = o

        attend(j, oth, store_other)
        c = remote(ob.at[j], ag.at[j, :, my_col], as_.at[j], ar.at[j], partner)
        go(None, c)
        a_copies.append(c)
        attend(j, own, store_own)

    h_copies = []
    pair_cols = pl.ds(pl.multiple_of(h * 2 * hc, 2 * hc), 2 * hc)

    def stage_d(j):
        a_copies[j].wait_recv()
        hcs = []
        for d, dev in enumerate(others):
            c = remote(ag.at[j, :, pair_cols], ag.at[j, :, pair_cols], hs.at[j, d], hr.at[j, d], dev)
            go(None, c)
            hcs.append(c)
        h_copies.append(hcs)
        pair = ag[j, :, pair_cols]
        att_ref[:, j * hc : (j + 1) * hc] = pair[:, :hc]
        att_ref[:, (per + j) * hc : (per + j + 1) * hc] = pair[:, hc:]

    def stage_e(j):
        for c in h_copies[j]:
            c.wait_recv()
        for c in w_copies[j]:
            c.wait()

        def body(t, carry):
            n = pl.ds(pl.multiple_of(t * 256, 256), 256)
            part = jnp.dot(ag[j], wb[j, :, n], preferred_element_type=jnp.float32)
            if j == 0:
                acc_ref[:, n] = part
            else:
                acc_ref[:, n] += part
            return carry

        lax.fori_loop(0, local // 256, body, 0)

    stages = [stage_a, stage_b, stage_c, stage_d, stage_e]
    for step in range(per + len(stages) - 1):
        for i, stage in enumerate(stages):
            if 0 <= step - i < per:
                stage(step - i)
    for cond, c in sends:
        run(cond, lambda c=c: c.wait_send())


def attention(q, k, v, w, lengths):
    n_tok, n_hid = lax.axis_size("tok"), lax.axis_size("hid")
    rows, local = q.shape
    per = local // HEAD_DIM // 2
    dma = pltpu.SemaphoreType.DMA
    any_ = pl.BlockSpec(memory_space=pl.ANY)
    vm = pl.BlockSpec(memory_space=pltpu.VMEM)
    bf = jnp.bfloat16
    return pl.pallas_call(
        functools.partial(attention_kernel, n_tok, n_hid, lengths.shape[0]),
        out_shape=(
            jax.ShapeDtypeStruct((rows, local), jnp.float32),
            jax.ShapeDtypeStruct((rows, local), bf),
        ),
        in_specs=[any_] * 4 + [pl.BlockSpec(memory_space=pltpu.SMEM)],
        out_specs=(vm, vm),
        scratch_shapes=[
            pltpu.VMEM((per, 2 * rows, HEAD_DIM), bf),
            pltpu.VMEM((per, 2, 8 * rows, HEAD_DIM), bf),
            pltpu.VMEM((per, rows, 2 * n_hid * HEAD_DIM), bf),
            pltpu.VMEM((per, 2 * n_hid * HEAD_DIM, local), bf),
            pltpu.VMEM((per, rows, HEAD_DIM), bf),
            dma((per, 2 * n_hid)),
            dma((per, 3)),
            dma((per, 3)),
            dma((per, 3)),
            dma((per, 2, 2)),
            dma((per, 2, 2)),
            dma((per, 2)),
            dma((per, 2)),
            dma((per, 2)),
            dma((per, 2)),
            dma((per,)),
            dma((per,)),
            dma((per, n_hid - 1)),
            dma((per, n_hid - 1)),
        ],
        compiler_params=pltpu.CompilerParams(
            collective_id=0, has_side_effects=True, vmem_limit_bytes=44 * 1024 * 1024
        ),
        cost_estimate=pl.CostEstimate(
            flops=6_000_000_000, bytes_accessed=200_000_000, transcendentals=5_000_000
        ),
        name="attention_project",
    )(q, k, v, w, lengths)


def finish_kernel(
    n_hid, requests, rank,
    acc_ref, att_ref, res_ref, maps_ref, scale_ref, shift_ref, len_ref,
    stream_ref, normed_ref,
    tot, db, sb, ds_, dr, ss_, sr,
):
    rows, local = acc_ref.shape
    tok, h = lax.axis_index("tok"), lax.axis_index("hid")
    others = [(tok, lax.rem(h + d, n_hid)) for d in range(1, n_hid)]
    greet([(None, o) for o in others])
    wide = requests * rank

    def exchange(buf, ssem, rsem):
        copies = []
        for d, dev in enumerate(others):
            c = pltpu.make_async_remote_copy(
                src_ref=buf.at[h], dst_ref=buf.at[h], send_sem=ssem.at[d], recv_sem=rsem.at[d],
                device_id=dev, device_id_type=MESH,
            )
            c.start()
            copies.append(c)
        return copies

    seg = segment_of(tok * rows + lax.broadcasted_iota(jnp.int32, (1, rows), 1), len_ref, requests)
    mine = lax.broadcasted_iota(jnp.int32, (wide, rows), 0) // rank == seg
    part = lax.dot_general(maps_ref[0:wide, :], att_ref[...], NT, preferred_element_type=jnp.float32)
    part = jnp.where(mine, part, 0.0)
    folded = part[0:rank, :]
    for r in range(1, requests):
        folded = folded + part[r * rank : (r + 1) * rank, :]
    db[h] = folded
    copies = exchange(db, ds_, dr)
    tot[...] = acc_ref[...] + res_ref[...].astype(jnp.float32)
    for c in copies:
        c.wait()
    down = db[0]
    for g in range(1, n_hid):
        down = down + db[g]
    down = jnp.concatenate([down] * requests, axis=0)
    expand = jnp.where(mine, down, 0.0).astype(jnp.bfloat16)
    lift = lax.dot_general(
        expand, maps_ref[wide : 2 * wide, :], (((0,), (0,)), ((), ())), preferred_element_type=jnp.float32
    )
    total = tot[...] + lift
    tot[...] = total
    mean = jnp.sum(total, axis=1, keepdims=True) / local
    off = total - mean
    square = jnp.sum(off * off, axis=1, keepdims=True)
    lane = lax.broadcasted_iota(jnp.int32, (rows, 128), 1)
    sb[h] = jnp.transpose(jnp.where(lane == 0, mean, square))[0:8, :]
    copies = exchange(sb, ss_, sr)
    stream_ref[...] = total.astype(jnp.bfloat16)
    for c in copies:
        c.wait()
    stats = [sb[g] for g in range(n_hid)]
    means = [s[0:1, :] for s in stats]
    mean = sum(means[1:], means[0]) / n_hid
    var = stats[0][1:2, :] + local * (means[0] - mean) * (means[0] - mean)
    for g in range(1, n_hid):
        var = var + stats[g][1:2, :] + local * (means[g] - mean) * (means[g] - mean)
    inv = 1.0 / jnp.sqrt(var / (local * n_hid) + 1e-06)
    row = lax.broadcasted_iota(jnp.int32, (128, rows), 0)
    back = jnp.transpose(jnp.where(row == 0, mean, inv))
    normed_ref[...] = (
        (tot[...] - back[:, 0:1]) * back[:, 1:2] * (1.0 + scale_ref[...]) + shift_ref[...]
    ).astype(jnp.bfloat16)


def finish(acc, att, residual, maps, scale, shift, lengths, rank):
    n_hid = lax.axis_size("hid")
    rows, local = acc.shape
    dma = pltpu.SemaphoreType.DMA
    vm = pl.BlockSpec(memory_space=pltpu.VMEM)
    return pl.pallas_call(
        functools.partial(finish_kernel, n_hid, lengths.shape[0], rank),
        out_shape=(jax.ShapeDtypeStruct((rows, local), jnp.bfloat16),) * 2,
        in_specs=[vm] * 6 + [pl.BlockSpec(memory_space=pltpu.SMEM)],
        out_specs=(vm, vm),
        scratch_shapes=[
            pltpu.VMEM((rows, local), jnp.float32),
            pltpu.VMEM((n_hid, rank, rows), jnp.float32),
            pltpu.VMEM((n_hid, 8, rows), jnp.float32),
            dma((n_hid - 1,)),
            dma((n_hid - 1,)),
            dma((n_hid - 1,)),
            dma((n_hid - 1,)),
        ],
        compiler_params=pltpu.CompilerParams(
            collective_id=1, has_side_effects=True, vmem_limit_bytes=32 * 1024 * 1024
        ),
        name="adapter_norm",
    )(acc, att, residual, maps, scale, shift, lengths)


def on_device(
    queries, keys, values, residual, out_weight, adapter_a, adapter_b,
    request_lengths, request_adapter, adapter_slot, mod_scale, mod_shift,
):
    held, local, rank = adapter_a.shape
    requests = request_lengths.shape[0]
    slots = adapter_slot[request_adapter] - lax.axis_index("tok") * held
    here = ((slots >= 0) & (slots < held))[:, None, None]
    slots = jnp.clip(slots, 0, held - 1)
    take = lambda bank: jnp.stack(
        [lax.dynamic_index_in_dim(bank, slots[r], 0, keepdims=False) for r in range(requests)]
    )
    a = jnp.where(here, jnp.transpose(take(adapter_a), (0, 2, 1)), 0)
    b = jnp.where(here, take(adapter_b), 0)
    maps = jnp.concatenate([a.reshape(requests * rank, local), b.reshape(requests * rank, local)], axis=0)
    maps = lax.psum(maps, "tok")
    acc, att = attention(queries, keys, values, out_weight, request_lengths)
    return finish(acc, att, residual, maps, mod_scale[None, :], mod_shift[None, :], request_lengths, rank)


def solution(mesh):
    placed = (
        P("tok", "hid"),
        P("tok", "hid"),
        P("tok", "hid"),
        P("tok", "hid"),
        P(None, "hid"),
        P("tok", "hid", None),
        P("tok", None, "hid"),
        P(),
        P(),
        P(),
        P("hid"),
        P("hid"),
    )
    return jax.shard_map(
        on_device,
        mesh=mesh,
        in_specs=placed,
        out_specs=(P("tok", "hid"), P("tok", "hid")),
        check_vma=False,
    )
```

```python
import functools
import math

import jax
import jax.numpy as jnp
from jax import lax
from jax.experimental import pallas as pl
from jax.experimental.pallas import tpu as pltpu
from jax.sharding import PartitionSpec as P

HEAD_DIM = 128
D = 5120
MESH = pl.DeviceIdType.MESH
NT = (((1,), (1,)), ((), ()))


def segment_of(pos, len_ref, requests):
    end = jnp.int32(0)
    seg = jnp.zeros_like(pos)
    for r in range(requests):
        end = end + len_ref[r]
        seg = seg + (pos >= end).astype(jnp.int32)
    return jnp.where(pos < 0, -1, seg)


def greet(targets):
    barrier = pltpu.get_barrier_semaphore()
    count = jnp.int32(0)
    for cond, dev in targets:

        def signal(dev=dev):
            pl.semaphore_signal(barrier, inc=1, device_id=dev, device_id_type=MESH)

        if cond is None:
            signal()
            count = count + 1
        else:
            pl.when(cond)(signal)
            count = count + cond.astype(jnp.int32)
    pl.semaphore_wait(barrier, count)


def run(cond, fn):
    if cond is None:
        fn()
    else:
        pl.when(cond)(fn)


def block_kernel(
    n_tok, n_hid, requests, rank,
    q_ref, k_ref, v_ref, w_ref, res_ref, a_ref, b_ref, scale_ref, shift_ref, len_ref, req_ref, slot_ref,
    stream_ref, normed_ref,
    qb, kv, ag, wb, ob, acc_ref, att_ref, mo, mi, cu, cd, fu, fd, tm, db, sb,
    w_sem, l_sem, ys, yr, zs, zr, ps, pr, fs, fr, as_, ar, hs, hr, ms, mr, ds_, dr, ss_, sr,
):
    rows, local = q_ref.shape
    hc = HEAD_DIM
    heads = local // hc
    per = (heads + 1) // 2
    second = heads - per
    tok, h = lax.axis_index("tok"), lax.axis_index("hid")
    p, y = tok // 2, tok % 2
    levels = n_tok // 2
    partner = (2 * p + 1 - y, h)
    up, down = (tok + 2, h), (tok - 2, h)
    has_up, has_down = p < levels - 1, p > 0
    others = [(tok, lax.rem(h + d, n_hid)) for d in range(1, n_hid)]
    greet([(None, partner), (has_up, up), (has_down, down)] + [(None, o) for o in others])

    own = pl.multiple_of(y * rows, rows)
    oth = pl.multiple_of((1 - y) * rows, rows)
    own_cols = y * (second * hc)
    oth_cols = (1 - y) * (second * hc)
    base = 3 * rows
    sends = []

    def remote(src, dst, ss, rs, dev):
        return pltpu.make_async_remote_copy(
            src_ref=src, dst_ref=dst, send_sem=ss, recv_sem=rs, device_id=dev, device_id_type=MESH
        )

    def go(cond, copy):
        run(cond, lambda: copy.start())
        sends.append((cond, copy))

    def cols(start, j):
        return pl.ds(pl.multiple_of(start + j * hc, hc), hc)

    ways = [(has_up, up, base - 2 * rows, has_down), (has_down, down, base + 2 * rows, has_up)]

    wide = requests * rank
    held = a_ref.shape[0]
    for i, bank in enumerate((a_ref, b_ref)):
        for r in range(requests):
            slot = slot_ref[req_ref[r]] - tok * held
            held_here = (slot >= 0) & (slot < held)
            got = bank[jnp.clip(slot, 0, held - 1)]
            mo[i, r * rank : (r + 1) * rank, :] = jnp.where(held_here, got, jnp.zeros_like(got))
    m_pair = remote(mo.at[1 - y], mi, ms.at[0], mr.at[0], partner)
    m_up = remote(fu, cu, ms.at[1], mr.at[1], up)
    m_down = remote(fd, cd, ms.at[2], mr.at[2], down)
    m_back = remote(tm.at[y], tm.at[y], ms.at[3], mr.at[3], partner)

    @pl.when(p == 0)
    def _():
        cu[...] = jnp.zeros_like(cu)

    @pl.when(p == levels - 1)
    def _():
        cd[...] = jnp.zeros_like(cd)

    chain_steps = 4

    def maps_at(step):
        if step == 0:
            m_pair.wait_recv()
            mi[...] = mi[...] + mo[y]
        if step < chain_steps:
            back = levels - 1 - p
            last = step == chain_steps - 1

            @pl.when((p >= step) if last else (p == step))
            def _():
                run(has_down, lambda: m_up.wait_recv())
                fu[...] = mi[...] + cu[...]
                run(has_up, lambda: m_up.start())

            @pl.when((back >= step) if last else (back == step))
            def _():
                run(has_up, lambda: m_down.wait_recv())
                fd[...] = mi[...] + cd[...]
                run(has_down, lambda: m_down.start())

        if step == chain_steps:
            tm[y] = mi[...] + cu[...] + cd[...]
            m_back.start()

    sends.extend([(None, m_pair), (has_up, m_up), (has_down, m_down), (None, m_back)])

    y_copies, l_copies, z_copies = [], [], []
    for j in range(per):
        yc, lc, zc = [], [], []
        for i, (ref, at) in enumerate(((k_ref, kv), (v_ref, kv), (q_ref, qb))):
            src = ref.at[:, cols(oth_cols, j)]
            mine = ref.at[:, cols(own_cols, j)]
            dst = kv.at[j, i, pl.ds(base + own, rows), :] if i < 2 else qb.at[j, pl.ds(own, rows), :]
            c = remote(src, dst, ys.at[j, i], yr.at[j, i], partner)
            go(None, c)
            yc.append(c)
            c = pltpu.make_async_copy(mine, dst, l_sem.at[j, i])
            c.start()
            lc.append(c)
            if i < 2:
                for w, (cond, dev, first, rcond) in enumerate(ways):
                    c = remote(
                        mine, kv.at[j, i, pl.ds(first + own, rows), :], zs.at[j, w, i], zr.at[j, w, i], dev
                    )
                    go(cond, c)
                    zc.append((rcond, c))
        y_copies.append(yc)
        l_copies.append(lc)
        z_copies.append(zc)

    m_pair.start()
    w_copies = []
    for j in range(per):
        wc = []
        for g in range(2 * n_hid):
            row = (g // 2) * local + (g % 2) * second * hc + j * hc
            if g % 2 == 1 and j < per - second:
                wb[j, g * hc : (g + 1) * hc, :] = jnp.zeros((hc, local), wb.dtype)
                continue
            c = pltpu.make_async_copy(
                w_ref.at[pl.ds(row, hc), :], wb.at[j, pl.ds(g * hc, hc), :], w_sem.at[j, g]
            )
            c.start()
            wc.append(c)
        w_copies.append(wc)

    @pl.when(p == 0)
    def _():
        kv[:, :, 0 : 3 * rows, :] = jnp.zeros((per, 2, 3 * rows, hc), kv.dtype)

    @pl.when(p == 1)
    def _():
        kv[:, :, 0:rows, :] = jnp.zeros((per, 2, rows, hc), kv.dtype)

    @pl.when(p == levels - 1)
    def _():
        kv[:, :, 5 * rows : 8 * rows, :] = jnp.zeros((per, 2, 3 * rows, hc), kv.dtype)

    @pl.when(p == levels - 2)
    def _():
        kv[:, :, 7 * rows : 8 * rows, :] = jnp.zeros((per, 2, rows, hc), kv.dtype)

    p_copies = []

    def stage_a(j):
        for c in y_copies[j]:
            c.wait_recv()
        pc = []
        for w, (cond, dev, first, rcond) in enumerate(ways):
            c = remote(
                kv.at[j, :, pl.ds(base + oth, rows), :],
                kv.at[j, :, pl.ds(first + oth, rows), :],
                ps.at[j, w], pr.at[j, w], dev,
            )
            go(cond, c)
            pc.append((rcond, c))
        p_copies.append(pc)

    f_copies = []
    fwd = [
        (has_up & has_down, up, 2 * rows, 0, p > 1),
        (has_up & has_down, down, 5 * rows, 7 * rows, p < levels - 2),
    ]

    def stage_b(j):
        fc = []
        for w, (cond, dev, src, dst, rcond) in enumerate(fwd):
            for rc, c in z_copies[j][w::2] + p_copies[j][w : w + 1]:
                run(rc, lambda c=c: c.wait_recv())
            c = remote(
                kv.at[j, :, pl.ds(src, rows), :], kv.at[j, :, pl.ds(dst, rows), :],
                fs.at[j, w], fr.at[j, w], dev,
            )
            go(cond, c)
            fc.append((rcond, c))
        f_copies.append(fc)

    wide_tile = 256 if local % 256 == 0 else 128
    scale = math.log2(math.e) / math.sqrt(HEAD_DIM)
    tile = 128
    span = 7 * rows

    def attend(j, first, store):
        level_pos = p * (2 * rows)
        kseg = segment_of(
            level_pos - base + first + lax.broadcasted_iota(jnp.int32, (1, span), 1), len_ref, requests
        )

        def body(t, carry):
            at = pl.multiple_of(t * tile, tile)
            qseg = segment_of(
                level_pos + first + at + lax.broadcasted_iota(jnp.int32, (tile, 1), 0), len_ref, requests
            )
            q = qb[j, pl.ds(first + at, tile), :]
            s = lax.dot_general(
                q, kv[j, 0, pl.ds(first, span), :], NT, preferred_element_type=jnp.float32
            )
            s = jnp.where(qseg == kseg, s, -1e30)
            top = jnp.max(s, axis=1, keepdims=True)
            e = jnp.exp2((s - top) * scale)
            total = jnp.sum(e, axis=1, keepdims=True)
            o = jnp.dot(
                e.astype(jnp.bfloat16), kv[j, 1, pl.ds(first, span), :], preferred_element_type=jnp.float32
            )
            store(at, (o / total).astype(jnp.bfloat16))
            return carry

        lax.fori_loop(0, rows // tile, body, 0)

    a_copies = []
    my_col = pl.ds(pl.multiple_of((h * 2 + y) * hc, hc), hc)

    def stage_c(j):
        for c in l_copies[j]:
            c.wait()
        for rc, c in f_copies[j]:
            run(rc, lambda c=c: c.wait_recv())

        def store_other(at, o):
            ob[j, pl.ds(at, tile), :] = o

        def store_own(at, o):
            ag[j, pl.ds(at, tile), my_col] = o

        attend(j, oth, store_other)
        c = remote(ob.at[j], ag.at[j, :, my_col], as_.at[j], ar.at[j], partner)
        go(None, c)
        a_copies.append(c)
        attend(j, own, store_own)

    h_copies, t_copies = [], []
    x, core, nx = h // 2, h % 2, n_hid // 2
    twin = (tok, x * 2 + 1 - core)
    pair_cols = pl.ds(pl.multiple_of(h * 2 * hc, 2 * hc), 2 * hc)

    def stage_d(j):
        a_copies[j].wait_recv()
        hcs = []
        for d in range(1, nx):
            dev = (tok, lax.rem(x + d, nx) * 2 + core)
            c = remote(ag.at[j, :, pair_cols], ag.at[j, :, pair_cols], hs.at[j, d], hr.at[j, d], dev)
            go(None, c)
            hcs.append(c)
        c = remote(ag.at[j, :, pair_cols], ag.at[j, :, pair_cols], hs.at[j, 0], hr.at[j, 0], twin)
        go(None, c)
        h_copies.append(hcs)
        t_copies.append([c])
        pair = ag[j, :, pair_cols]
        att_ref[:, j * hc : (j + 1) * hc] = pair[:, :hc]
        att_ref[:, (second + j) * hc : (second + j + 1) * hc] = pair[:, hc:]

    def stage_t(j):
        for d in range(1, nx):
            h_copies[j][d - 1].wait_recv()
            there = lax.rem(x - d + nx, nx) * 2 + core
            at = pl.ds(pl.multiple_of(there * 2 * hc, 2 * hc), 2 * hc)
            c = remote(ag.at[j, :, at], ag.at[j, :, at], hs.at[j, nx - 1 + d], hr.at[j, nx - 1 + d], twin)
            go(None, c)
            t_copies[j].append(c)

    def stage_e(j):
        for c in t_copies[j]:
            c.wait_recv()
        for c in w_copies[j]:
            c.wait()

        def body(t, carry):
            n = pl.ds(pl.multiple_of(t * wide_tile, wide_tile), wide_tile)
            part = jnp.dot(ag[j], wb[j, :, n], preferred_element_type=jnp.float32)
            if j == 0:
                acc_ref[:, n] = part
            else:
                acc_ref[:, n] += part
            return carry

        lax.fori_loop(0, local // wide_tile, body, 0)

    def exchange(buf, ssem, rsem):
        copies = []
        for d, dev in enumerate(others):
            c = pltpu.make_async_remote_copy(
                src_ref=buf.at[h], dst_ref=buf.at[h], send_sem=ssem.at[d], recv_sem=rsem.at[d],
                device_id=dev, device_id_type=MESH,
            )
            c.start()
            copies.append(c)
        return copies

    def adapter_down():
        seg = segment_of(tok * rows + lax.broadcasted_iota(jnp.int32, (1, rows), 1), len_ref, requests)
        mine = lax.broadcasted_iota(jnp.int32, (wide, rows), 0) // rank == seg
        part = lax.dot_general(tm[0], att_ref[...], NT, preferred_element_type=jnp.float32)
        part = jnp.where(mine, part, 0.0)
        folded = part[0:rank, :]
        for r in range(1, requests):
            folded = folded + part[r * rank : (r + 1) * rank, :]
        db[h] = folded
        return mine, exchange(db, ds_, dr)

    stages = [stage_a, stage_b, stage_c, stage_d, stage_t, stage_e]
    for step in range(per + len(stages) - 1):
        for i, stage in enumerate(stages):
            if 0 <= step - i < per:
                stage(step - i)
            if i == 3 and step - i == per - 1:
                m_back.wait_recv()
                mine, copies = adapter_down()
        maps_at(step)
    for c in copies:
        c.wait()
    down = db[0]
    for g in range(1, n_hid):
        down = down + db[g]
    down = jnp.concatenate([down] * requests, axis=0)
    expand = jnp.where(mine, down, 0.0).astype(jnp.bfloat16)
    lift = lax.dot_general(
        expand, tm[1], (((0,), (0,)), ((), ())), preferred_element_type=jnp.float32
    )
    total = acc_ref[...] + res_ref[...].astype(jnp.float32) + lift
    acc_ref[...] = total
    mean = jnp.sum(total, axis=1, keepdims=True) / local
    off = total - mean
    square = jnp.sum(off * off, axis=1, keepdims=True)
    lane = lax.broadcasted_iota(jnp.int32, (rows, 128), 1)
    sb[h] = jnp.transpose(jnp.where(lane == 0, mean, square))[0:8, :]
    copies = exchange(sb, ss_, sr)
    stream_ref[...] = total.astype(jnp.bfloat16)
    for c in copies:
        c.wait()
    stats = [sb[g] for g in range(n_hid)]
    means = [s[0:1, :] for s in stats]
    mean = sum(means[1:], means[0]) / n_hid
    var = stats[0][1:2, :] + local * (means[0] - mean) * (means[0] - mean)
    for g in range(1, n_hid):
        var = var + stats[g][1:2, :] + local * (means[g] - mean) * (means[g] - mean)
    inv = 1.0 / jnp.sqrt(var / (local * n_hid) + 1e-06)
    row = lax.broadcasted_iota(jnp.int32, (128, rows), 0)
    back = jnp.transpose(jnp.where(row == 0, mean, inv))
    normed_ref[...] = (
        (acc_ref[...] - back[:, 0:1]) * back[:, 1:2] * (1.0 + scale_ref[...]) + shift_ref[...]
    ).astype(jnp.bfloat16)
    for cond, c in sends:
        run(cond, lambda c=c: c.wait_send())


def block(q, k, v, w, residual, bank_a, bank_b, scale, shift, lengths, adapters, slots):
    n_tok, n_hid = lax.axis_size("tok"), lax.axis_size("hid")
    rows, local = q.shape
    rank = bank_a.shape[1]
    requests = lengths.shape[0]
    per = (local // HEAD_DIM + 1) // 2
    dma = pltpu.SemaphoreType.DMA
    hbm = pl.BlockSpec(memory_space=pltpu.HBM)
    vm = pl.BlockSpec(memory_space=pltpu.VMEM)
    sm = pl.BlockSpec(memory_space=pltpu.SMEM)
    bf = jnp.bfloat16
    maps = pltpu.VMEM((requests * rank, local), bf)
    pair = pltpu.VMEM((2, requests * rank, local), bf)
    return pl.pallas_call(
        functools.partial(block_kernel, n_tok, n_hid, requests, rank),
        out_shape=(jax.ShapeDtypeStruct((rows, local), bf),) * 2,
        in_specs=[hbm] * 4 + [vm] * 5 + [sm] * 3,
        out_specs=(vm, vm),
        scratch_shapes=[
            pltpu.VMEM((per, 2 * rows, HEAD_DIM), bf),
            pltpu.VMEM((per, 2, 8 * rows, HEAD_DIM), bf),
            pltpu.VMEM((per, rows, 2 * n_hid * HEAD_DIM), bf),
            pltpu.VMEM((per, 2 * n_hid * HEAD_DIM, local), bf),
            pltpu.VMEM((per, rows, HEAD_DIM), bf),
            pltpu.VMEM((rows, local), jnp.float32),
            pltpu.VMEM((rows, local), bf),
            pair, maps, maps, maps, maps, maps, pair,
            pltpu.VMEM((n_hid, rank, rows), jnp.float32),
            pltpu.VMEM((n_hid, 8, rows), jnp.float32),
            dma((per, 2 * n_hid)),
            dma((per, 3)),
            dma((per, 3)),
            dma((per, 3)),
            dma((per, 2, 2)),
            dma((per, 2, 2)),
            dma((per, 2)),
            dma((per, 2)),
            dma((per, 2)),
            dma((per, 2)),
            dma((per,)),
            dma((per,)),
            dma((per, n_hid)),
            dma((per, n_hid)),
            dma((4,)),
            dma((4,)),
            dma((n_hid - 1,)),
            dma((n_hid - 1,)),
            dma((n_hid - 1,)),
            dma((n_hid - 1,)),
        ],
        compiler_params=pltpu.CompilerParams(
            collective_id=0, has_side_effects=True, vmem_limit_bytes=48 * 1024 * 1024
        ),
        name="block",
    )(q, k, v, w, residual, bank_a, bank_b, scale, shift, lengths, adapters, slots)


def on_device(
    queries, keys, values, residual, out_weight, adapter_a, adapter_b,
    request_lengths, request_adapter, adapter_slot, mod_scale, mod_shift,
):
    return block(
        queries, keys, values, out_weight, residual, jnp.transpose(adapter_a, (0, 2, 1)), adapter_b,
        mod_scale[None, :], mod_shift[None, :], request_lengths, request_adapter, adapter_slot,
    )


def solution(mesh):
    placed = (
        P("tok", "hid"),
        P("tok", "hid"),
        P("tok", "hid"),
        P("tok", "hid"),
        P(None, "hid"),
        P("tok", "hid", None),
        P("tok", None, "hid"),
        P(),
        P(),
        P(),
        P("hid"),
        P("hid"),
    )
    return jax.shard_map(
        on_device,
        mesh=mesh,
        in_specs=placed,
        out_specs=(P("tok", "hid"), P("tok", "hid")),
        check_vma=False,
    )
```

```python
import functools
import math

import jax
import jax.numpy as jnp
from jax import lax
from jax.experimental import pallas as pl
from jax.experimental.pallas import tpu as pltpu
from jax.sharding import PartitionSpec as P

HEAD_DIM = 128
D = 5120
MESH = pl.DeviceIdType.MESH
NT = (((1,), (1,)), ((), ()))


def segment_of(pos, len_ref, requests):
    end = jnp.int32(0)
    seg = jnp.zeros_like(pos)
    for r in range(requests):
        end = end + len_ref[r]
        seg = seg + (pos >= end).astype(jnp.int32)
    return jnp.where(pos < 0, -1, seg)


def greet(targets):
    barrier = pltpu.get_barrier_semaphore()
    count = jnp.int32(0)
    for cond, dev in targets:

        def signal(dev=dev):
            pl.semaphore_signal(barrier, inc=1, device_id=dev, device_id_type=MESH)

        if cond is None:
            signal()
            count = count + 1
        else:
            pl.when(cond)(signal)
            count = count + cond.astype(jnp.int32)
    pl.semaphore_wait(barrier, count)


def run(cond, fn):
    if cond is None:
        fn()
    else:
        pl.when(cond)(fn)


def block_kernel(
    n_tok, n_hid, requests, rank,
    q_ref, k_ref, v_ref, w_ref, res_ref, a_ref, b_ref, scale_ref, shift_ref, len_ref, req_ref, slot_ref,
    stream_ref, normed_ref,
    qb, kv, ag, wb, ob, acc_ref, att_ref, mo, mi, cu, cd, fu, fd, tm, db, sb,
    w_sem, l_sem, ys, yr, zs, zr, ps, pr, fs, fr, as_, ar, hs, hr, ms, mr, ds_, dr, ss_, sr, i_sem, a_buf, b_buf, res_buf,
):
    rows, local = q_ref.shape
    hc = HEAD_DIM
    heads = local // hc
    per = (heads + 1) // 2
    second = heads - per
    tok, h = lax.axis_index("tok"), lax.axis_index("hid")
    p, y = tok // 2, tok % 2
    levels = n_tok // 2
    partner = (2 * p + 1 - y, h)
    up, down = (tok + 2, h), (tok - 2, h)
    has_up, has_down = p < levels - 1, p > 0
    others = [(tok, lax.rem(h + d, n_hid)) for d in range(1, n_hid)]
    greet([(None, partner), (has_up, up), (has_down, down)] + [(None, o) for o in others])

    own = pl.multiple_of(y * rows, rows)
    oth = pl.multiple_of((1 - y) * rows, rows)
    own_cols = y * (second * hc)
    oth_cols = (1 - y) * (second * hc)
    base = 3 * rows
    sends = []

    def remote(src, dst, ss, rs, dev):
        return pltpu.make_async_remote_copy(
            src_ref=src, dst_ref=dst, send_sem=ss, recv_sem=rs, device_id=dev, device_id_type=MESH
        )

    def go(cond, copy):
        run(cond, lambda: copy.start())
        sends.append((cond, copy))

    def cols(start, j):
        return pl.ds(pl.multiple_of(start + j * hc, hc), hc)

    ways = [(has_up, up, base - 2 * rows, has_down), (has_down, down, base + 2 * rows, has_up)]

    b_copies = [
        pltpu.make_async_copy(src, dst, i_sem.at[i]) for i, (src, dst) in enumerate(((a_ref, a_buf), (b_ref, b_buf)))
    ]
    r_copy = pltpu.make_async_copy(res_ref, res_buf, i_sem.at[2])
    for c in b_copies:
        c.start()

    wide = requests * rank
    held = a_ref.shape[0]

    def adapter_maps():
        for c in b_copies:
            c.wait()
        for i, bank in enumerate((a_buf, b_buf)):
            for r in range(requests):
                slot = slot_ref[req_ref[r]] - tok * held
                held_here = (slot >= 0) & (slot < held)
                got = bank[jnp.clip(slot, 0, held - 1)]
                mo[i, r * rank : (r + 1) * rank, :] = jnp.where(held_here, got, jnp.zeros_like(got))
        m_pair.start()

    m_pair = remote(mo.at[1 - y], mi, ms.at[0], mr.at[0], partner)
    m_up = remote(fu, cu, ms.at[1], mr.at[1], up)
    m_down = remote(fd, cd, ms.at[2], mr.at[2], down)
    m_back = remote(tm.at[y], tm.at[y], ms.at[3], mr.at[3], partner)

    @pl.when(p == 0)
    def _():
        cu[...] = jnp.zeros_like(cu)

    @pl.when(p == levels - 1)
    def _():
        cd[...] = jnp.zeros_like(cd)

    chain_steps = 4

    def maps_at(step):
        if step == 0:
            m_pair.wait_recv()
            mi[...] = mi[...] + mo[y]
        if step < chain_steps:
            back = levels - 1 - p
            last = step == chain_steps - 1

            @pl.when((p >= step) if last else (p == step))
            def _():
                run(has_down, lambda: m_up.wait_recv())
                fu[...] = mi[...] + cu[...]
                run(has_up, lambda: m_up.start())

            @pl.when((back >= step) if last else (back == step))
            def _():
                run(has_up, lambda: m_down.wait_recv())
                fd[...] = mi[...] + cd[...]
                run(has_down, lambda: m_down.start())

        if step == chain_steps:
            tm[y] = mi[...] + cu[...] + cd[...]
            m_back.start()

    sends.extend([(None, m_pair), (has_up, m_up), (has_down, m_down), (None, m_back)])

    y_copies, l_copies, z_copies, w_copies = [], [], [], []

    def stage_s(j):
        yc, lc, zc = [], [], []
        for i, (ref, at) in enumerate(((k_ref, kv), (v_ref, kv), (q_ref, qb))):
            src = ref.at[:, cols(oth_cols, j)]
            mine = ref.at[:, cols(own_cols, j)]
            dst = kv.at[j, i, pl.ds(base + own, rows), :] if i < 2 else qb.at[j, pl.ds(own, rows), :]
            c = remote(src, dst, ys.at[j, i], yr.at[j, i], partner)
            go(None, c)
            yc.append(c)
            c = pltpu.make_async_copy(mine, dst, l_sem.at[j, i])
            c.start()
            lc.append(c)
            if i < 2:
                for w, (cond, dev, first, rcond) in enumerate(ways):
                    c = remote(
                        mine, kv.at[j, i, pl.ds(first + own, rows), :], zs.at[j, w, i], zr.at[j, w, i], dev
                    )
                    go(cond, c)
                    zc.append((rcond, c))
        y_copies.append(yc)
        l_copies.append(lc)
        z_copies.append(zc)

    def stage_w(j):
        wc = []
        for g in range(2 * n_hid):
            row = (g // 2) * local + (g % 2) * second * hc + j * hc
            if g % 2 == 1 and j < per - second:
                wb[j, g * hc : (g + 1) * hc, :] = jnp.zeros((hc, local), wb.dtype)
                continue
            c = pltpu.make_async_copy(
                w_ref.at[pl.ds(row, hc), :], wb.at[j, pl.ds(g * hc, hc), :], w_sem.at[j, g]
            )
            c.start()
            wc.append(c)
        w_copies.append(wc)

    ahead = 2
    for j in range(min(ahead, per)):
        stage_s(j)
    adapter_maps()

    @pl.when(p == 0)
    def _():
        kv[:, :, 0 : 3 * rows, :] = jnp.zeros((per, 2, 3 * rows, hc), kv.dtype)

    @pl.when(p == 1)
    def _():
        kv[:, :, 0:rows, :] = jnp.zeros((per, 2, rows, hc), kv.dtype)

    @pl.when(p == levels - 1)
    def _():
        kv[:, :, 5 * rows : 8 * rows, :] = jnp.zeros((per, 2, 3 * rows, hc), kv.dtype)

    @pl.when(p == levels - 2)
    def _():
        kv[:, :, 7 * rows : 8 * rows, :] = jnp.zeros((per, 2, rows, hc), kv.dtype)

    p_copies = []

    def stage_a(j):
        for c in y_copies[j]:
            c.wait_recv()
        pc = []
        for w, (cond, dev, first, rcond) in enumerate(ways):
            c = remote(
                kv.at[j, :, pl.ds(base + oth, rows), :],
                kv.at[j, :, pl.ds(first + oth, rows), :],
                ps.at[j, w], pr.at[j, w], dev,
            )
            go(cond, c)
            pc.append((rcond, c))
        p_copies.append(pc)

    f_copies = []
    fwd = [
        (has_up & has_down, up, 2 * rows, 0, p > 1),
        (has_up & has_down, down, 5 * rows, 7 * rows, p < levels - 2),
    ]

    def stage_b(j):
        fc = []
        for w, (cond, dev, src, dst, rcond) in enumerate(fwd):
            for rc, c in z_copies[j][w::2] + p_copies[j][w : w + 1]:
                run(rc, lambda c=c: c.wait_recv())
            c = remote(
                kv.at[j, :, pl.ds(src, rows), :], kv.at[j, :, pl.ds(dst, rows), :],
                fs.at[j, w], fr.at[j, w], dev,
            )
            go(cond, c)
            fc.append((rcond, c))
        f_copies.append(fc)

    wide_tile = 256 if local % 256 == 0 else 128
    scale = math.log2(math.e) / math.sqrt(HEAD_DIM)
    tile = 128
    span = 7 * rows

    def attend(j, first, store):
        level_pos = p * (2 * rows)
        kseg = segment_of(
            level_pos - base + first + lax.broadcasted_iota(jnp.int32, (1, span), 1), len_ref, requests
        )

        def body(t, carry):
            at = pl.multiple_of(t * tile, tile)
            qseg = segment_of(
                level_pos + first + at + lax.broadcasted_iota(jnp.int32, (tile, 1), 0), len_ref, requests
            )
            q = qb[j, pl.ds(first + at, tile), :]
            s = lax.dot_general(
                q, kv[j, 0, pl.ds(first, span), :], NT, preferred_element_type=jnp.float32
            )
            s = jnp.where(qseg == kseg, s, -1e30)
            top = jnp.max(s, axis=1, keepdims=True)
            e = jnp.exp2((s - top) * scale)
            total = jnp.sum(e, axis=1, keepdims=True)
            o = jnp.dot(
                e.astype(jnp.bfloat16), kv[j, 1, pl.ds(first, span), :], preferred_element_type=jnp.float32
            )
            store(at, (o / total).astype(jnp.bfloat16))
            return carry

        lax.fori_loop(0, rows // tile, body, 0)

    a_copies = []
    my_col = pl.ds(pl.multiple_of((h * 2 + y) * hc, hc), hc)

    def stage_c(j):
        for c in l_copies[j]:
            c.wait()
        for rc, c in f_copies[j]:
            run(rc, lambda c=c: c.wait_recv())

        def store_other(at, o):
            ob[j, pl.ds(at, tile), :] = o

        def store_own(at, o):
            ag[j, pl.ds(at, tile), my_col] = o

        attend(j, oth, store_other)
        c = remote(ob.at[j], ag.at[j, :, my_col], as_.at[j], ar.at[j], partner)
        go(None, c)
        a_copies.append(c)
        attend(j, own, store_own)

    h_copies, t_copies = [], []
    x, core, nx = h // 2, h % 2, n_hid // 2
    twin = (tok, x * 2 + 1 - core)
    pair_cols = pl.ds(pl.multiple_of(h * 2 * hc, 2 * hc), 2 * hc)

    def stage_d(j):
        a_copies[j].wait_recv()
        hcs = []
        for d in range(1, nx):
            dev = (tok, lax.rem(x + d, nx) * 2 + core)
            c = remote(ag.at[j, :, pair_cols], ag.at[j, :, pair_cols], hs.at[j, d], hr.at[j, d], dev)
            go(None, c)
            hcs.append(c)
        c = remote(ag.at[j, :, pair_cols], ag.at[j, :, pair_cols], hs.at[j, 0], hr.at[j, 0], twin)
        go(None, c)
        h_copies.append(hcs)
        t_copies.append([c])
        pair = ag[j, :, pair_cols]
        att_ref[:, j * hc : (j + 1) * hc] = pair[:, :hc]
        att_ref[:, (second + j) * hc : (second + j + 1) * hc] = pair[:, hc:]

    def stage_t(j):
        for d in range(1, nx):
            h_copies[j][d - 1].wait_recv()
            there = lax.rem(x - d + nx, nx) * 2 + core
            at = pl.ds(pl.multiple_of(there * 2 * hc, 2 * hc), 2 * hc)
            c = remote(ag.at[j, :, at], ag.at[j, :, at], hs.at[j, nx - 1 + d], hr.at[j, nx - 1 + d], twin)
            go(None, c)
            t_copies[j].append(c)

    def stage_e(j):
        for c in t_copies[j]:
            c.wait_recv()
        for c in w_copies[j]:
            c.wait()

        def body(t, carry):
            n = pl.ds(pl.multiple_of(t * wide_tile, wide_tile), wide_tile)
            part = jnp.dot(ag[j], wb[j, :, n], preferred_element_type=jnp.float32)
            if j == 0:
                acc_ref[:, n] = part
            else:
                acc_ref[:, n] += part
            return carry

        lax.fori_loop(0, local // wide_tile, body, 0)

    def exchange(buf, ssem, rsem):
        copies = []
        for d, dev in enumerate(others):
            c = pltpu.make_async_remote_copy(
                src_ref=buf.at[h], dst_ref=buf.at[h], send_sem=ssem.at[d], recv_sem=rsem.at[d],
                device_id=dev, device_id_type=MESH,
            )
            c.start()
            copies.append(c)
        return copies

    def adapter_down():
        seg = segment_of(tok * rows + lax.broadcasted_iota(jnp.int32, (1, rows), 1), len_ref, requests)
        mine = lax.broadcasted_iota(jnp.int32, (wide, rows), 0) // rank == seg
        part = lax.dot_general(tm[0], att_ref[...], NT, preferred_element_type=jnp.float32)
        part = jnp.where(mine, part, 0.0)
        folded = part[0:rank, :]
        for r in range(1, requests):
            folded = folded + part[r * rank : (r + 1) * rank, :]
        db[h] = folded
        return mine, exchange(db, ds_, dr)

    stages = [stage_a, stage_b, stage_c, stage_d, stage_t, stage_e]
    for step in range(per + len(stages) - 1):
        for i, stage in enumerate(stages):
            if 0 <= step - i < per:
                stage(step - i)
            if i == 0 and step < per:
                if step + ahead < per:
                    stage_s(step + ahead)
                stage_w(step)
                if step == per - 1:
                    r_copy.start()
            if i == 3 and step - i == per - 1:
                m_back.wait_recv()
                mine, copies = adapter_down()
        maps_at(step)
    for c in copies:
        c.wait()
    down = db[0]
    for g in range(1, n_hid):
        down = down + db[g]
    down = jnp.concatenate([down] * requests, axis=0)
    expand = jnp.where(mine, down, 0.0).astype(jnp.bfloat16)
    lift = lax.dot_general(
        expand, tm[1], (((0,), (0,)), ((), ())), preferred_element_type=jnp.float32
    )
    r_copy.wait()
    total = acc_ref[...] + res_buf[...].astype(jnp.float32) + lift
    acc_ref[...] = total
    mean = jnp.sum(total, axis=1, keepdims=True) / local
    off = total - mean
    square = jnp.sum(off * off, axis=1, keepdims=True)
    lane = lax.broadcasted_iota(jnp.int32, (rows, 128), 1)
    sb[h] = jnp.transpose(jnp.where(lane == 0, mean, square))[0:8, :]
    copies = exchange(sb, ss_, sr)
    stream_ref[...] = total.astype(jnp.bfloat16)
    for c in copies:
        c.wait()
    stats = [sb[g] for g in range(n_hid)]
    means = [s[0:1, :] for s in stats]
    mean = sum(means[1:], means[0]) / n_hid
    var = stats[0][1:2, :] + local * (means[0] - mean) * (means[0] - mean)
    for g in range(1, n_hid):
        var = var + stats[g][1:2, :] + local * (means[g] - mean) * (means[g] - mean)
    inv = 1.0 / jnp.sqrt(var / (local * n_hid) + 1e-06)
    row = lax.broadcasted_iota(jnp.int32, (128, rows), 0)
    back = jnp.transpose(jnp.where(row == 0, mean, inv))
    normed_ref[...] = (
        (acc_ref[...] - back[:, 0:1]) * back[:, 1:2] * (1.0 + scale_ref[...].reshape(1, local)) + shift_ref[...].reshape(1, local)
    ).astype(jnp.bfloat16)
    for cond, c in sends:
        run(cond, lambda c=c: c.wait_send())


def block(q, k, v, w, residual, bank_a, bank_b, scale, shift, lengths, adapters, slots):
    n_tok, n_hid = lax.axis_size("tok"), lax.axis_size("hid")
    rows, local = q.shape
    rank = bank_a.shape[1]
    requests = lengths.shape[0]
    per = (local // HEAD_DIM + 1) // 2
    dma = pltpu.SemaphoreType.DMA
    hbm = pl.BlockSpec(memory_space=pltpu.HBM)
    vm = pl.BlockSpec(memory_space=pltpu.VMEM)
    sm = pl.BlockSpec(memory_space=pltpu.SMEM)
    bf = jnp.bfloat16
    maps = pltpu.VMEM((requests * rank, local), bf)
    pair = pltpu.VMEM((2, requests * rank, local), bf)
    return pl.pallas_call(
        functools.partial(block_kernel, n_tok, n_hid, requests, rank),
        out_shape=(jax.ShapeDtypeStruct((rows, local), bf),) * 2,
        in_specs=[hbm] * 7 + [vm] * 2 + [sm] * 3,
        out_specs=(vm, vm),
        scratch_shapes=[
            pltpu.VMEM((per, 2 * rows, HEAD_DIM), bf),
            pltpu.VMEM((per, 2, 8 * rows, HEAD_DIM), bf),
            pltpu.VMEM((per, rows, 2 * n_hid * HEAD_DIM), bf),
            pltpu.VMEM((per, 2 * n_hid * HEAD_DIM, local), bf),
            pltpu.VMEM((per, rows, HEAD_DIM), bf),
            pltpu.VMEM((rows, local), jnp.float32),
            pltpu.VMEM((rows, local), bf),
            pair, maps, maps, maps, maps, maps, pair,
            pltpu.VMEM((n_hid, rank, rows), jnp.float32),
            pltpu.VMEM((n_hid, 8, rows), jnp.float32),
            dma((per, 2 * n_hid)),
            dma((per, 3)),
            dma((per, 3)),
            dma((per, 3)),
            dma((per, 2, 2)),
            dma((per, 2, 2)),
            dma((per, 2)),
            dma((per, 2)),
            dma((per, 2)),
            dma((per, 2)),
            dma((per,)),
            dma((per,)),
            dma((per, n_hid)),
            dma((per, n_hid)),
            dma((4,)),
            dma((4,)),
            dma((n_hid - 1,)),
            dma((n_hid - 1,)),
            dma((n_hid - 1,)),
            dma((n_hid - 1,)),
            dma((3,)),
            pltpu.VMEM(bank_a.shape, bf),
            pltpu.VMEM(bank_b.shape, bf),
            pltpu.VMEM((rows, local), bf),
        ],
        compiler_params=pltpu.CompilerParams(
            collective_id=0, has_side_effects=True, vmem_limit_bytes=60 * 1024 * 1024
        ),
        name="block",
    )(q, k, v, w, residual, bank_a, bank_b, scale, shift, lengths, adapters, slots)


def on_device(
    queries, keys, values, residual, out_weight, adapter_a, adapter_b,
    request_lengths, request_adapter, adapter_slot, mod_scale, mod_shift,
):
    return block(
        queries, keys, values, out_weight, residual, jnp.transpose(adapter_a, (0, 2, 1)), adapter_b,
        mod_scale, mod_shift, request_lengths, request_adapter, adapter_slot,
    )


def solution(mesh):
    placed = (
        P("tok", "hid"),
        P("tok", "hid"),
        P("tok", "hid"),
        P("tok", "hid"),
        P(None, "hid"),
        P("tok", "hid", None),
        P("tok", None, "hid"),
        P(),
        P(),
        P(),
        P("hid"),
        P("hid"),
    )
    return jax.shard_map(
        on_device,
        mesh=mesh,
        in_specs=placed,
        out_specs=(P("tok", "hid"), P("tok", "hid")),
        check_vma=False,
    )
```
